128 devices in a mesh: slab: 8 (over x, core), tile: 16 (over z, y).
Axes of the slice: x: 4, y: 4, z: 4, core: 2. Of those that a mesh axis runs over, the one named last changes fastest.
Arguments:
- soil_diag: float32 [4096, 128, 128], P(('slab', 'tile'))
- soil_off: float32 [4096, 4, 128, 128], P(('slab', 'tile')), may hold values from -0.3125 to 0.3125
- soil_pre: float32 [4096, 128, 128], P(('slab', 'tile'))
- own_cols: int32 [4096, 2], P(('slab', 'tile')), may hold values from 0 to 31
- margin_slot: int32 [4096], P(('slab', 'tile')), may hold values from 0 to 31
- vertical_col: int32 [4096], P(('slab', 'tile')), may hold values from 0 to 63, as said below
- fetch_rows: int32 [128, 16, 2], P(('slab', 'tile')), may hold values from 0 to 31
- soil_rhs: float32 [4096, 128], P(('slab', 'tile')), may hold values from -6 to 6
- root_diag: float32 [1024, 128, 128], P(('slab', 'tile'))
- root_pre: float32 [1024, 128, 128], P(('slab', 'tile'))
- root_up: float32 [1024, 128, 128], P(('slab', 'tile')), may hold values from -0.3125 to 0.3125
- root_down: float32 [1024, 128, 128], P(('slab', 'tile')), may hold values from -0.3125 to 0.3125
- root_cell: int32 [1024], P(('slab', 'tile')), may hold values from 0 to 31
- root_count: int32 [128], P(('slab', 'tile')), may hold values from 1 to 8, as said below
- root_rhs: float32 [1024, 128], P(('slab', 'tile')), may hold values from -6 to 6
Outputs:
- soil_solution: float32 [4096, 128], P(('slab', 'tile'))
- root_solution: float32 [1024, 128], P(('slab', 'tile'))
- soil_residual: float32 [4096, 128], P(('slab', 'tile'))
The draws below stay inside these ranges and needn't reach their ends.
Inputs may be any that keep to these rules, and one draw needn't show every extreme that they name: `fetch_rows`: entry [d, p, c] names a block of the brick in the same slab at tile p. `vertical_col`: values below 32 couple to the slab beneath, others to the slab above; rows of the first slab always couple upward and of the last slab downward. `root_count`: some brick has all 8 slots live.
All inputs are finite; a program needn't handle non-finite values.
Results may differ from the reference program's by a relative error of at most 0.00014.
Values sent between devices are 32-bit elements; how exact they have to be, the bound alone decides.
No kernel may reach another device: no remote copies, remote signals or barrier semaphores. Data moves between devices by JAX's collectives and lax.ppermute only.
A program may use at most 64 MiB of HBM per device.

```python
import jax
import jax.numpy as jnp
from jax import lax

B = 128
NBD = 32
RCAP = 8
CAP = 2
SWEEPS = 3
NB_ALL = 4096
R_ALL = 1024
SLOTS = 32
N_SLAB = 8
N_TILE = 16
DEVICES = 128


def dominant(noise, diag_key, count, low, high, spread):
    diag = jax.random.uniform(diag_key, (count, B), jnp.float32, low, high)
    return noise * (spread / B ** 0.5) + jnp.eye(B, dtype=jnp.float32)[None] * diag[:, :, None]


def draw_soil_diag(key, part):
    key = jax.random.fold_in(key, 3)
    noise_key, diag_key = jax.random.split(key)
    noise = jax.random.normal(noise_key, (NB_ALL, B, B), jnp.float32)
    return dominant(noise, diag_key, NB_ALL, 2.0, 4.0, 0.5)


def draw_soil_pre(key, part):
    key = jax.random.fold_in(key, 5)
    noise_key, diag_key = jax.random.split(key)
    noise = jax.random.normal(noise_key, (NB_ALL, B, B), jnp.float32)
    return dominant(noise, diag_key, NB_ALL, 0.25, 0.5, 0.1)


def draw_root_diag(key, part):
    key = jax.random.fold_in(key, 9)
    noise_key, diag_key = jax.random.split(key)
    noise = jax.random.normal(noise_key, (R_ALL, B, B), jnp.float32)
    return dominant(noise, diag_key, R_ALL, 2.0, 4.0, 0.5)


def draw_root_pre(key, part):
    key = jax.random.fold_in(key, 13)
    noise_key, diag_key = jax.random.split(key)
    noise = jax.random.normal(noise_key, (R_ALL, B, B), jnp.float32)
    return dominant(noise, diag_key, R_ALL, 0.25, 0.5, 0.1)


def draw_vertical_col(key, part):
    key = jax.random.fold_in(key, 11)
    side_key, place_key = jax.random.split(key)
    slab = jnp.arange(NB_ALL, dtype=jnp.int32) // NBD // N_TILE
    side = jax.random.randint(side_key, (NB_ALL,), 0, 2, dtype=jnp.int32)
    side = jnp.where(slab == 0, 1, jnp.where(slab == N_SLAB - 1, 0, side))
    place = jax.random.randint(place_key, (NB_ALL,), 0, NBD, dtype=jnp.int32)
    return (side * NBD + place).astype(jnp.int32)


def draw_root_count(key, part):
    key = jax.random.fold_in(key, 7)
    count_key, full_key = jax.random.split(key)
    counts = jax.random.randint(count_key, (DEVICES,), 1, RCAP + 1, dtype=jnp.int32)
    full = jax.random.randint(full_key, (), 0, DEVICES, dtype=jnp.int32)
    return counts.at[full].set(RCAP).astype(jnp.int32)


def with_ends(values, rng, smallest, largest):
    index_at = [jax.random.randint(jax.random.fold_in(rng, axis), (), 0, length) for axis, length in enumerate(values.shape)]
    main_axis = values.shape.index(max(values.shape))
    next_to = index_at[:main_axis] + [(index_at[main_axis] + 1) % values.shape[main_axis]] + index_at[main_axis + 1:]
    return values.at[tuple(index_at)].set(smallest).at[tuple(next_to)].set(largest)


def shard_levels(own_key, dims, pieces, smallest, largest):
    loudness, own = 1.0, jax.random.fold_in(own_key, 6)
    for dim, blocks in pieces:
        heights = jnp.exp(jax.random.uniform(jax.random.fold_in(own, dim), (blocks,), jnp.float32, smallest / len(pieces), largest / len(pieces)))
        loudness = loudness * jnp.repeat(heights, dims[dim] // blocks).reshape([-1 if axis == dim else 1 for axis in range(len(dims))])
    return loudness


def scatter_about(key, shape, scale, limit, shards=(), kind=jnp.bfloat16):
    result = jax.random.normal(key, shape, jnp.float32) * scale
    if len(shards) > 0:
        result = shard_levels(key, shape, shards, -0.22, 0.18) * result
    return jnp.clip(result, min=-limit, max=limit).astype(kind)


def setup_inputs(seed: int = 0) -> dict:
    streams_of = jax.random.split(jax.random.key(seed), 16)
    soil_diag = draw_soil_diag(jax.random.fold_in(streams_of[15], 71), 0)
    soil_off = scatter_about(streams_of[1], (NB_ALL, 4, B, B), (0.25 / B ** 0.5), 0.3125, ((0, 128),), jnp.float32)
    soil_pre = draw_soil_pre(jax.random.fold_in(streams_of[15], 71), 0)
    own_cols = with_ends(jax.random.randint(streams_of[3], (NB_ALL, 2), 0, NBD), jax.random.fold_in(streams_of[3], 1), 0, NBD - 1).astype(jnp.int32)
    margin_slot = with_ends(jax.random.randint(streams_of[4], (NB_ALL,), 0, SLOTS), jax.random.fold_in(streams_of[4], 1), 0, SLOTS - 1).astype(jnp.int32)
    vertical_col = draw_vertical_col(jax.random.fold_in(streams_of[15], 71), 0)
    fetch_rows = with_ends(jax.random.randint(streams_of[6], (DEVICES, N_TILE, CAP), 0, NBD), jax.random.fold_in(streams_of[6], 1), 0, NBD - 1).astype(jnp.int32)
    soil_rhs = scatter_about(streams_of[7], (NB_ALL, B), 1.0, 6.0, ((0, 128),), jnp.float32)
    root_diag = draw_root_diag(jax.random.fold_in(streams_of[15], 71), 0)
    root_pre = draw_root_pre(jax.random.fold_in(streams_of[15], 71), 0)
    root_up = scatter_about(streams_of[10], (R_ALL, B, B), (0.25 / B ** 0.5), 0.3125, ((0, 128),), jnp.float32)
    root_down = scatter_about(streams_of[11], (R_ALL, B, B), (0.25 / B ** 0.5), 0.3125, ((0, 128),), jnp.float32)
    root_cell = with_ends(jax.random.randint(streams_of[12], (R_ALL,), 0, NBD), jax.random.fold_in(streams_of[12], 1), 0, NBD - 1).astype(jnp.int32)
    root_count = draw_root_count(jax.random.fold_in(streams_of[15], 71), 0)
    root_rhs = scatter_about(streams_of[14], (R_ALL, B), 1.0, 6.0, ((0, 128),), jnp.float32)
    return dict(soil_diag=soil_diag, soil_off=soil_off, soil_pre=soil_pre, own_cols=own_cols, margin_slot=margin_slot, vertical_col=vertical_col, fetch_rows=fetch_rows, soil_rhs=soil_rhs, root_diag=root_diag, root_pre=root_pre, root_up=root_up, root_down=root_down, root_cell=root_cell, root_count=root_count, root_rhs=root_rhs)


LOW_BOUND = 0.25
HIGH_BOUND = 2.0


def blocks(mats, vecs):
    return jnp.einsum("nij,nj->ni", mats, vecs, precision=lax.Precision.HIGHEST)


def reference(soil_diag, soil_off, soil_pre, own_cols, margin_slot, vertical_col, fetch_rows, soil_rhs, root_diag, root_pre, root_up, root_down, root_cell, root_count, root_rhs):
    total = soil_rhs.shape[0]
    rows = jnp.arange(total, dtype=jnp.int32)
    device = rows // NBD
    slab = device // N_TILE
    tile = device % N_TILE
    first = device * NBD + own_cols[:, 0]
    second = device * NBD + own_cols[:, 1]
    peer = margin_slot // CAP
    place = margin_slot % CAP
    margin = (slab * N_TILE + peer) * NBD + fetch_rows[device, peer, place]
    other_slab = jnp.where(vertical_col < NBD, slab - 1, slab + 1)
    vertical = (other_slab * N_TILE + tile) * NBD + vertical_col % NBD
    cols = jnp.stack([first, second, margin, vertical], axis=1).astype(jnp.int32)
    keep = jnp.array([1.0, 1.0, 1.0, 0.0], dtype=jnp.float32)
    root_total = root_rhs.shape[0]
    root_rows = jnp.arange(root_total, dtype=jnp.int32)
    root_dev = root_rows // RCAP
    live = (root_rows % RCAP < root_count[root_dev]).astype(jnp.float32)
    cell_global = (root_dev * NBD + root_cell).astype(jnp.int32)

    def operate(soil_vec, root_vec):
        near = soil_vec[cols]
        soil_out = blocks(soil_diag, soil_vec) + jnp.einsum("nkij,nkj->ni", soil_off, near, precision=lax.Precision.HIGHEST)
        down = blocks(root_down, root_vec) * live[:, None]
        soil_out = soil_out.at[cell_global].add(down)
        root_out = live[:, None] * (blocks(root_diag, root_vec) + blocks(root_up, soil_vec[cell_global]))
        return soil_out, root_out

    def precond(soil_res, root_res):
        first_turn = blocks(soil_pre, soil_res)
        near = first_turn[cols] * keep[None, :, None]
        extended = blocks(soil_diag, first_turn) + jnp.einsum("nkij,nkj->ni", soil_off, near, precision=lax.Precision.HIGHEST)
        soil_out = first_turn + blocks(soil_pre, soil_res - extended)
        root_out = live[:, None] * blocks(root_pre, root_res)
        return soil_out, root_out

    theta = (HIGH_BOUND + LOW_BOUND) / 2.0
    delta = (HIGH_BOUND - LOW_BOUND) / 2.0
    sigma = theta / delta
    rho = 1.0 / sigma
    soil_x = jnp.zeros_like(soil_rhs)
    root_x = jnp.zeros_like(root_rhs)
    soil_r = soil_rhs
    root_r = live[:, None] * root_rhs
    soil_z, root_z = precond(soil_r, root_r)
    soil_step = soil_z / theta
    root_step = root_z / theta
    for sweep in range(SWEEPS):
        soil_x = soil_x + soil_step
        root_x = root_x + root_step
        soil_a, root_a = operate(soil_step, root_step)
        soil_r = soil_r - soil_a
        root_r = root_r - root_a
        if sweep + 1 < SWEEPS:
            rho_new = 1.0 / (2.0 * sigma - rho)
            soil_z, root_z = precond(soil_r, root_r)
            soil_step = rho_new * rho * soil_step + (2.0 * rho_new / delta) * soil_z
            root_step = rho_new * rho * root_step + (2.0 * rho_new / delta) * root_z
            rho = rho_new
    return soil_x, root_x, soil_r
```

```python
import functools

import jax
import jax.numpy as jnp
from jax import lax
from jax.experimental import pallas as pl
from jax.experimental.pallas import tpu as pltpu
from jax.sharding import PartitionSpec as P

SWEEPS = 3
LOW_BOUND = 0.25
HIGH_BOUND = 2.0
THETA = (HIGH_BOUND + LOW_BOUND) / 2.0
DELTA = (HIGH_BOUND - LOW_BOUND) / 2.0
SIGMA = THETA / DELTA

B = 128
NBD = 32
RCAP = 8
TILES = 16
CAP = 2
SLOTS = TILES * CAP
PIECE = NBD + 8
F32 = jnp.float32

VMEM = pl.BlockSpec(memory_space=pltpu.VMEM)
SMEM = pl.BlockSpec(memory_space=pltpu.SMEM)


def row_sum(acc):
    lane = lax.broadcasted_iota(jnp.int32, (8, B), 1)
    sub = lax.broadcasted_iota(jnp.int32, (8, B), 0)
    ahead = lane - sub
    sums = jnp.sum(acc.reshape(B // 8, 8, B), axis=2, keepdims=True)
    out = jnp.zeros((8, B), F32)
    for k in range(B // 8):
        out = jnp.where(ahead == 8 * k, sums[k], out)
    return jnp.sum(out, axis=0, keepdims=True)


def product(*pairs):
    acc = None
    for mat, vec in pairs:
        term = mat * vec
        acc = term if acc is None else acc + term
    return row_sum(acc)


def row(ref, index):
    return ref[pl.ds(index, 1), :]


def pick(choice, values):
    return jnp.dot(
        choice[:, :NBD], values, precision=lax.Precision.HIGHEST, preferred_element_type=F32
    )


def first_kernel(fetch, pre, rhs, t_out, send):
    for g in range(NBD):
        t_out[g : g + 1, :] = product((pre[g], rhs[g : g + 1, :]))
    t = t_out[...]
    sub = lax.broadcasted_iota(jnp.int32, (8, B), 0)
    for p in range(TILES):
        send[p, :NBD, :] = t
        asked = jnp.where(sub == 0, fetch[0, p, 0], fetch[0, p, 1])
        send[p, NBD:, :] = asked.astype(F32)


def extended_rows(own, near_row, diag, off, pre, t, res, w):
    for g in range(NBD):
        w[g : g + 1, :] = res[g : g + 1, :] - product(
            (diag[g], t[g : g + 1, :]),
            (off[g, 0], row(t, own[g, 0])),
            (off[g, 1], row(t, own[g, 1])),
            (off[g, 2], near_row(g)),
        )


def first_step_kernel(
    own, margin, fetch, count, diag, off, pre, t, table, rhs, root_pre, root_rhs,
    s_out, send, choice, ur_out, w,
):
    def near_row(g):
        slot = margin[g]
        peer = slot // CAP
        return table[peer, pl.ds(fetch[0, peer, slot % CAP], 1), :]

    extended_rows(own, near_row, diag, off, pre, t, rhs, w)
    for g in range(NBD):
        z = t[g : g + 1, :] + product((pre[g], w[g : g + 1, :]))
        s_out[g : g + 1, :] = z * (1.0 / THETA)
    lane = lax.broadcasted_iota(jnp.int32, (CAP, B), 1).astype(F32)
    for p in range(TILES):
        choice[CAP * p : CAP * (p + 1), :] = (table[p, NBD : NBD + CAP, :] == lane).astype(F32)
    send[...] = pick(choice[...], s_out[...])
    for r in range(RCAP):
        z = product((root_pre[r], root_rhs[r : r + 1, :]))
        ur_out[r : r + 1, :] = jnp.where(r < count[0], z * (1.0 / THETA), 0.0)


def step_kernel(
    keep, gain, own, margin, diag, off, pre, t, table, res, s_in, x_in, choice,
    s_out, x_out, send, w,
):
    extended_rows(own, lambda g: row(table, margin[g]), diag, off, pre, t, res, w)
    for g in range(NBD):
        z = t[g : g + 1, :] + product((pre[g], w[g : g + 1, :]))
        s = keep * s_in[g : g + 1, :] + gain * z
        s_out[g : g + 1, :] = s
        x_out[g : g + 1, :] = x_in[g : g + 1, :] + s
    send[...] = pick(choice[...], s_out[...])


def residual_rows(own, margin, vert, odd, cell, diag, off, down, s, table, core, chip, res, ur, r_out):
    r_out[...] = res[...]
    for r in range(RCAP):
        at = pl.ds(cell[r], 1)
        r_out[at, :] = r_out[at, :] - product((down[r], ur[r : r + 1, :]))
    for g in range(NBD):
        place = vert[g] % NBD
        below = (vert[g] < NBD).astype(jnp.int32)
        over = jnp.where(below == odd[0], row(core, place), row(chip, place))
        r_out[g : g + 1, :] = r_out[g : g + 1, :] - product(
            (diag[g], s[g : g + 1, :]),
            (off[g, 0], row(s, own[g, 0])),
            (off[g, 1], row(s, own[g, 1])),
            (off[g, 2], row(table, margin[g])),
            (off[g, 3], over),
        )


def residual_kernel(
    keep, gain, own, margin, vert, odd, cell, count,
    diag, off, pre, root_diag, root_pre, root_up, down,
    s, table, core, chip, res, ur, rr, root_x, choice,
    t_out, r_out, ur_out, rr_out, root_x_out, send,
):
    residual_rows(own, margin, vert, odd, cell, diag, off, down, s, table, core, chip, res, ur, r_out)
    for g in range(NBD):
        t_out[g : g + 1, :] = product((pre[g], r_out[g : g + 1, :]))
    send[...] = pick(choice[...], t_out[...])
    for r in range(RCAP):
        change = product((root_diag[r], ur[r : r + 1, :]), (root_up[r], row(s, cell[r])))
        rr_out[r : r + 1, :] = rr[r : r + 1, :] - change
    for r in range(RCAP):
        z = product((root_pre[r], rr_out[r : r + 1, :]))
        new = jnp.where(r < count[0], keep * ur[r : r + 1, :] + gain * z, 0.0)
        ur_out[r : r + 1, :] = new
        root_x_out[r : r + 1, :] = root_x[r : r + 1, :] + new


def last_kernel(
    own, margin, vert, odd, cell, diag, off, down, s, table, core, chip, res, ur, r_out
):
    residual_rows(own, margin, vert, odd, cell, diag, off, down, s, table, core, chip, res, ur, r_out)


def call(kernel, name, scalars, arrays, outs, scratch=()):
    return pl.pallas_call(
        kernel,
        out_shape=tuple(jax.ShapeDtypeStruct(shape, F32) for shape in outs),
        in_specs=[SMEM] * len(scalars) + [VMEM] * len(arrays),
        out_specs=(VMEM,) * len(outs),
        scratch_shapes=[pltpu.VMEM(shape, F32) for shape in scratch],
        compiler_params=pltpu.CompilerParams(vmem_limit_bytes=4 * 2**20),
        name=name,
    )(*scalars, *arrays)


def body(
    soil_diag, soil_off, soil_pre, own_cols, margin_slot, vertical_col, fetch_rows, soil_rhs,
    root_diag, root_pre, root_up, root_down, root_cell, root_count, root_rhs,
):
    slabs = lax.axis_size("slab")
    odd = (lax.axis_index("slab") % 2).astype(jnp.int32).reshape(1)
    soil, root, table = (NBD, B), (RCAP, B), (SLOTS, B)

    def exchange(rows):
        got = lax.all_to_all(rows.reshape(TILES, CAP, B), "tile", 0, 0)
        return got.reshape(SLOTS, B)

    def vertical(s):
        core = lax.ppermute(s, "slab", [(i, i ^ 1) for i in range(slabs)])
        up = [(i, i + 1) for i in range(1, slabs - 1, 2)]
        chip = lax.ppermute(s, "slab", up + [(j, i) for i, j in up])
        return core, chip

    t, send = call(
        first_kernel, "first", (fetch_rows,), (soil_pre, soil_rhs), (soil, (TILES, PIECE, B))
    )
    got = lax.all_to_all(send, "tile", 0, 0)
    s, send, choice, ur = call(
        first_step_kernel, "step0",
        (own_cols, margin_slot, fetch_rows, root_count),
        (soil_diag, soil_off, soil_pre, t, got, soil_rhs, root_pre, root_rhs),
        (soil, table, table, root), (soil,),
    )
    x, r, rr, root_x = s, soil_rhs, root_rhs, ur
    rho = 1.0 / SIGMA
    for sweep in range(SWEEPS):
        core, chip = vertical(s)
        got = exchange(send)
        scalars = (own_cols, margin_slot, vertical_col, odd, root_cell)
        if sweep + 1 == SWEEPS:
            (r,) = call(
                last_kernel, "last", scalars,
                (soil_diag, soil_off, root_down, s, got, core, chip, r, ur), (soil,),
            )
            break
        rho_new = 1.0 / (2.0 * SIGMA - rho)
        keep, gain = rho_new * rho, 2.0 * rho_new / DELTA
        rho = rho_new
        t, r, ur, rr, root_x, send = call(
            functools.partial(residual_kernel, keep, gain), f"residual{sweep}",
            scalars + (root_count,),
            (soil_diag, soil_off, soil_pre, root_diag, root_pre, root_up, root_down,
             s, got, core, chip, r, ur, rr, root_x, choice),
            (soil, soil, root, root, root, table),
        )
        got = exchange(send)
        s, x, send = call(
            functools.partial(step_kernel, keep, gain), f"step{sweep + 1}",
            (own_cols, margin_slot),
            (soil_diag, soil_off, soil_pre, t, got, r, s, x, choice),
            (soil, soil, table), (soil,),
        )
    return x, root_x, r


def solution(mesh):
    split = P(("slab", "tile"))
    return jax.shard_map(
        body, mesh=mesh, in_specs=(split,) * 15, out_specs=(split,) * 3, check_vma=False
    )
```

```python
import functools

import jax
import jax.numpy as jnp
from jax import lax
from jax.experimental import pallas as pl
from jax.experimental.pallas import tpu as pltpu
from jax.sharding import PartitionSpec as P

SWEEPS = 3
LOW_BOUND = 0.25
HIGH_BOUND = 2.0
THETA = (HIGH_BOUND + LOW_BOUND) / 2.0
DELTA = (HIGH_BOUND - LOW_BOUND) / 2.0
SIGMA = THETA / DELTA

B = 128
NBD = 32
RCAP = 8
TILES = 16
CAP = 2
SLOTS = TILES * CAP
PIECE = NBD + 8
F32 = jnp.float32

VMEM = pl.BlockSpec(memory_space=pltpu.VMEM)
SMEM = pl.BlockSpec(memory_space=pltpu.SMEM)


def row_sum(acc):
    lane = lax.broadcasted_iota(jnp.int32, (8, B), 1)
    sub = lax.broadcasted_iota(jnp.int32, (8, B), 0)
    ahead = lane - sub
    sums = jnp.sum(acc.reshape(B // 8, 8, B), axis=2, keepdims=True)
    out = jnp.zeros((8, B), F32)
    for k in range(B // 8):
        out = jnp.where(ahead == 8 * k, sums[k], out)
    return jnp.sum(out, axis=0, keepdims=True)


def product(*pairs):
    acc = None
    for mat, vec in pairs:
        term = mat * vec
        acc = term if acc is None else acc + term
    return row_sum(acc)


def row(ref, index):
    return ref[pl.ds(index, 1), :]


def pick(choice, values):
    return jnp.dot(
        choice[:, :NBD], values, precision=lax.Precision.HIGHEST, preferred_element_type=F32
    )


def first_kernel(fetch, pre, rhs, t_out, send):
    for g in range(NBD):
        t_out[g : g + 1, :] = product((pre[g], rhs[g : g + 1, :]))
    t = t_out[...]
    sub = lax.broadcasted_iota(jnp.int32, (8, B), 0)
    for p in range(TILES):
        send[p, :NBD, :] = t
        asked = jnp.where(sub == 0, fetch[0, 0, p], fetch[0, 1, p])
        send[p, NBD:, :] = asked.astype(F32)


def extended_rows(own, near_row, diag, off, pre, t, res, w):
    for g in range(NBD):
        w[g : g + 1, :] = res[g : g + 1, :] - product(
            (diag[g], t[g : g + 1, :]),
            (off[g, 0], row(t, own[0, g])),
            (off[g, 1], row(t, own[1, g])),
            (off[g, 2], near_row(g)),
        )


def first_step_kernel(
    own, margin, fetch, count, diag, off, pre, t, table, rhs, root_pre, root_rhs,
    s_out, send, choice, ur_out, w,
):
    def near_row(g):
        slot = margin[g]
        peer = slot // CAP
        return table[peer, pl.ds(fetch[0, slot % CAP, peer], 1), :]

    extended_rows(own, near_row, diag, off, pre, t, rhs, w)
    for g in range(NBD):
        z = t[g : g + 1, :] + product((pre[g], w[g : g + 1, :]))
        s_out[g : g + 1, :] = z * (1.0 / THETA)
    lane = lax.broadcasted_iota(jnp.int32, (CAP, B), 1).astype(F32)
    for p in range(TILES):
        choice[CAP * p : CAP * (p + 1), :] = (table[p, NBD : NBD + CAP, :] == lane).astype(F32)
    send[...] = pick(choice[...], s_out[...])
    for r in range(RCAP):
        z = product((root_pre[r], root_rhs[r : r + 1, :]))
        ur_out[r : r + 1, :] = jnp.where(r < count[0], z * (1.0 / THETA), 0.0)


def step_kernel(
    keep, gain, own, margin, diag, off, pre, t, table, res, s_in, x_in, choice,
    s_out, x_out, send, w,
):
    extended_rows(own, lambda g: row(table, margin[g]), diag, off, pre, t, res, w)
    for g in range(NBD):
        z = t[g : g + 1, :] + product((pre[g], w[g : g + 1, :]))
        s = keep * s_in[g : g + 1, :] + gain * z
        s_out[g : g + 1, :] = s
        x_out[g : g + 1, :] = x_in[g : g + 1, :] + s
    send[...] = pick(choice[...], s_out[...])


def residual_rows(own, margin, vert, odd, cell, diag, off, down, s, table, core, chip, res, ur, r_out):
    r_out[...] = res[...]
    for r in range(RCAP):
        at = pl.ds(cell[r], 1)
        r_out[at, :] = r_out[at, :] - product((down[r], ur[r : r + 1, :]))
    for g in range(NBD):
        place = vert[g] % NBD
        below = (vert[g] < NBD).astype(jnp.int32)
        over = jnp.where(below == odd[0], row(core, place), row(chip, place))
        r_out[g : g + 1, :] = r_out[g : g + 1, :] - product(
            (diag[g], s[g : g + 1, :]),
            (off[g, 0], row(s, own[0, g])),
            (off[g, 1], row(s, own[1, g])),
            (off[g, 2], row(table, margin[g])),
            (off[g, 3], over),
        )


def residual_kernel(
    keep, gain, own, margin, vert, odd, cell, count,
    diag, off, pre, root_diag, root_pre, root_up, down,
    s, table, core, chip, res, ur, rr, root_x, choice,
    t_out, r_out, ur_out, rr_out, root_x_out, send,
):
    residual_rows(own, margin, vert, odd, cell, diag, off, down, s, table, core, chip, res, ur, r_out)
    for g in range(NBD):
        t_out[g : g + 1, :] = product((pre[g], r_out[g : g + 1, :]))
    send[...] = pick(choice[...], t_out[...])
    for r in range(RCAP):
        change = product((root_diag[r], ur[r : r + 1, :]), (root_up[r], row(s, cell[r])))
        rr_out[r : r + 1, :] = rr[r : r + 1, :] - change
    for r in range(RCAP):
        z = product((root_pre[r], rr_out[r : r + 1, :]))
        new = jnp.where(r < count[0], keep * ur[r : r + 1, :] + gain * z, 0.0)
        ur_out[r : r + 1, :] = new
        root_x_out[r : r + 1, :] = root_x[r : r + 1, :] + new


def last_kernel(
    own, margin, vert, odd, cell, diag, off, down, s, table, core, chip, res, ur, r_out
):
    residual_rows(own, margin, vert, odd, cell, diag, off, down, s, table, core, chip, res, ur, r_out)


def call(kernel, name, scalars, arrays, outs, scratch=()):
    return pl.pallas_call(
        kernel,
        out_shape=tuple(jax.ShapeDtypeStruct(shape, F32) for shape in outs),
        in_specs=[SMEM] * len(scalars) + [VMEM] * len(arrays),
        out_specs=(VMEM,) * len(outs),
        scratch_shapes=list(scratch),
        compiler_params=pltpu.CompilerParams(vmem_limit_bytes=4 * 2**20),
        cost_estimate=pl.CostEstimate(
            flops=20_000_000_000, transcendentals=0, bytes_accessed=40_000_000
        ),
        name=name,
    )(*scalars, *arrays)


def body(
    soil_diag, soil_off, soil_pre, own_cols, margin_slot, vertical_col, fetch_rows, soil_rhs,
    root_diag, root_pre, root_up, root_down, root_cell, root_count, root_rhs,
):
    slabs = lax.axis_size("slab")
    odd = (lax.axis_index("slab") % 2).astype(jnp.int32).reshape(1)
    own_cols, fetch_rows = own_cols.T, jnp.swapaxes(fetch_rows, 1, 2)
    soil, root, table = (NBD, B), (RCAP, B), (SLOTS, B)

    def exchange(rows):
        got = lax.all_to_all(rows.reshape(TILES, CAP, B), "tile", 0, 0)
        return got.reshape(SLOTS, B)

    def vertical(s):
        core = lax.ppermute(s, "slab", [(i, i ^ 1) for i in range(slabs)])
        up = [(i, i + 1) for i in range(1, slabs - 1, 2)]
        chip = lax.ppermute(s, "slab", up + [(j, i) for i, j in up])
        return core, chip

    t, send = call(
        first_kernel, "first", (fetch_rows,), (soil_pre, soil_rhs), (soil, (TILES, PIECE, B))
    )
    got = lax.all_to_all(send, "tile", 0, 0)
    s, send, choice, ur = call(
        first_step_kernel, "step0",
        (own_cols, margin_slot, fetch_rows, root_count),
        (soil_diag, soil_off, soil_pre, t, got, soil_rhs, root_pre, root_rhs),
        (soil, table, table, root), (pltpu.VMEM(soil, F32),),
    )
    x, r, rr, root_x = s, soil_rhs, root_rhs, ur
    rho = 1.0 / SIGMA
    for sweep in range(SWEEPS):
        core, chip = vertical(s)
        got = exchange(send)
        scalars = (own_cols, margin_slot, vertical_col, odd, root_cell)
        if sweep + 1 == SWEEPS:
            (r,) = call(
                last_kernel, "last", scalars,
                (soil_diag, soil_off, root_down, s, got, core, chip, r, ur), (soil,),
            )
            break
        rho_new = 1.0 / (2.0 * SIGMA - rho)
        keep, gain = rho_new * rho, 2.0 * rho_new / DELTA
        rho = rho_new
        t, r, ur, rr, root_x, send = call(
            functools.partial(residual_kernel, keep, gain), f"residual{sweep}",
            scalars + (root_count,),
            (soil_diag, soil_off, soil_pre, root_diag, root_pre, root_up, root_down,
             s, got, core, chip, r, ur, rr, root_x, choice),
            (soil, soil, root, root, root, table),
        )
        got = exchange(send)
        s, x, send = call(
            functools.partial(step_kernel, keep, gain), f"step{sweep + 1}",
            (own_cols, margin_slot),
            (soil_diag, soil_off, soil_pre, t, got, r, s, x, choice),
            (soil, soil, table), (pltpu.VMEM(soil, F32),),
        )
    return x, root_x, r


def solution(mesh):
    split = P(("slab", "tile"))
    return jax.shard_map(
        body, mesh=mesh, in_specs=(split,) * 15, out_specs=(split,) * 3, check_vma=False
    )
```

```python
import functools

import jax
import jax.numpy as jnp
from jax import lax
from jax.experimental import pallas as pl
from jax.experimental.pallas import tpu as pltpu
from jax.sharding import PartitionSpec as P

SWEEPS = 3
LOW_BOUND = 0.25
HIGH_BOUND = 2.0
THETA = (HIGH_BOUND + LOW_BOUND) / 2.0
DELTA = (HIGH_BOUND - LOW_BOUND) / 2.0
SIGMA = THETA / DELTA

B = 128
NBD = 32
RCAP = 8
TILES = 16
CAP = 2
SLOTS = TILES * CAP
PIECE = NBD + 8
F32 = jnp.float32

VMEM = pl.BlockSpec(memory_space=pltpu.VMEM)
SMEM = pl.BlockSpec(memory_space=pltpu.SMEM)


def row_sum(acc):
    lane = lax.broadcasted_iota(jnp.int32, (8, B), 1)
    sub = lax.broadcasted_iota(jnp.int32, (8, B), 0)
    ahead = lane - sub
    sums = jnp.sum(acc.reshape(B // 8, 8, B), axis=2, keepdims=True)
    out = jnp.zeros((8, B), F32)
    for k in range(B // 8):
        out = jnp.where(ahead == 8 * k, sums[k], out)
    return jnp.sum(out, axis=0, keepdims=True)


def product(*pairs):
    acc = None
    for mat, vec in pairs:
        term = mat * vec
        acc = term if acc is None else acc + term
    return row_sum(acc)


def row(ref, index):
    return ref[pl.ds(index, 1), :]


def pick(choice, values):
    return jnp.dot(
        choice[:, :NBD], values, precision=lax.Precision.HIGHEST, preferred_element_type=F32
    )


def first_kernel(fetch, count, pre, rhs, t_out, send):
    for g in range(NBD):
        t_out[g : g + 1, :] = product((pre[g], rhs[g : g + 1, :]))
    t = t_out[...]
    sub = lax.broadcasted_iota(jnp.int32, (8, B), 0)
    for p in range(TILES):
        send[p, :NBD, :] = t
        asked = jnp.where(sub == 0, fetch[0, 0, p], fetch[0, 1, p])
        send[p, NBD:, :] = asked.astype(F32)


def extended_rows(own, near_row, diag, off, pre, t, res, w):
    for g in range(NBD):
        w[g : g + 1, :] = res[g : g + 1, :] - product(
            (diag[g], t[g : g + 1, :]),
            (off[g, 0], row(t, own[0, g])),
            (off[g, 1], row(t, own[1, g])),
            (off[g, 2], near_row(g)),
        )


def first_step_kernel(
    own, margin, fetch, count, diag, off, pre, t, table, rhs, root_pre, root_rhs,
    s_out, send, choice, ur_out, w,
):
    def near_row(g):
        slot = margin[g]
        peer = slot // CAP
        return table[peer, pl.ds(fetch[0, slot % CAP, peer], 1), :]

    extended_rows(own, near_row, diag, off, pre, t, rhs, w)
    for g in range(NBD):
        z = t[g : g + 1, :] + product((pre[g], w[g : g + 1, :]))
        s_out[g : g + 1, :] = z * (1.0 / THETA)
    lane = lax.broadcasted_iota(jnp.int32, (CAP, B), 1).astype(F32)
    for p in range(TILES):
        choice[CAP * p : CAP * (p + 1), :] = (table[p, NBD : NBD + CAP, :] == lane).astype(F32)
    send[...] = pick(choice[...], s_out[...])
    for r in range(RCAP):
        z = product((root_pre[r], root_rhs[r : r + 1, :]))
        ur_out[r : r + 1, :] = jnp.where(r < count[0], z * (1.0 / THETA), 0.0)


def step_kernel(
    keep, gain, own, margin, diag, off, pre, t, table, res, s_in, x_in, choice,
    s_out, x_out, send, w,
):
    extended_rows(own, lambda g: row(table, margin[g]), diag, off, pre, t, res, w)
    for g in range(NBD):
        z = t[g : g + 1, :] + product((pre[g], w[g : g + 1, :]))
        s = keep * s_in[g : g + 1, :] + gain * z
        s_out[g : g + 1, :] = s
        x_out[g : g + 1, :] = x_in[g : g + 1, :] + s
    send[...] = pick(choice[...], s_out[...])


def residual_rows(own, margin, vert, cell, diag, off, down, s, table, below, above, res, ur, r_out):
    r_out[...] = res[...]
    for r in range(RCAP):
        at = pl.ds(cell[r], 1)
        r_out[at, :] = r_out[at, :] - product((down[r], ur[r : r + 1, :]))
    for g in range(NBD):
        place = vert[g] % NBD
        over = jnp.where(vert[g] < NBD, row(below, place), row(above, place))
        r_out[g : g + 1, :] = r_out[g : g + 1, :] - product(
            (diag[g], s[g : g + 1, :]),
            (off[g, 0], row(s, own[0, g])),
            (off[g, 1], row(s, own[1, g])),
            (off[g, 2], row(table, margin[g])),
            (off[g, 3], over),
        )


def residual_kernel(
    keep, gain, own, margin, vert, cell, count,
    diag, off, pre, root_diag, root_pre, root_up, down,
    s, table, below, above, res, ur, rr, root_x, choice,
    t_out, r_out, ur_out, rr_out, root_x_out, send,
):
    residual_rows(own, margin, vert, cell, diag, off, down, s, table, below, above, res, ur, r_out)
    for g in range(NBD):
        t_out[g : g + 1, :] = product((pre[g], r_out[g : g + 1, :]))
    send[...] = pick(choice[...], t_out[...])
    for r in range(RCAP):
        change = product((root_diag[r], ur[r : r + 1, :]), (root_up[r], row(s, cell[r])))
        rr_out[r : r + 1, :] = rr[r : r + 1, :] - change
    for r in range(RCAP):
        z = product((root_pre[r], rr_out[r : r + 1, :]))
        new = jnp.where(r < count[0], keep * ur[r : r + 1, :] + gain * z, 0.0)
        ur_out[r : r + 1, :] = new
        root_x_out[r : r + 1, :] = root_x[r : r + 1, :] + new


def last_kernel(
    own, margin, vert, cell, diag, off, down, s, table, below, above, res, ur, r_out
):
    residual_rows(own, margin, vert, cell, diag, off, down, s, table, below, above, res, ur, r_out)


def call(kernel, name, scalars, arrays, outs, scratch=()):
    return pl.pallas_call(
        kernel,
        out_shape=tuple(jax.ShapeDtypeStruct(shape, F32) for shape in outs),
        in_specs=[SMEM] * len(scalars) + [VMEM] * len(arrays),
        out_specs=(VMEM,) * len(outs),
        scratch_shapes=list(scratch),
        compiler_params=pltpu.CompilerParams(vmem_limit_bytes=4 * 2**20),
        cost_estimate=pl.CostEstimate(
            flops=20_000_000_000, transcendentals=0, bytes_accessed=40_000_000
        ),
        name=name,
    )(*scalars, *arrays)


def body(
    soil_diag, soil_off, soil_pre, own_cols, margin_slot, vertical_col, fetch_rows, soil_rhs,
    root_diag, root_pre, root_up, root_down, root_cell, root_count, root_rhs,
):
    slabs = lax.axis_size("slab")
    own_cols, fetch_rows = own_cols.T, jnp.swapaxes(fetch_rows, 1, 2)
    soil, root, table = (NBD, B), (RCAP, B), (SLOTS, B)

    def exchange(rows):
        got = lax.all_to_all(rows.reshape(TILES, CAP, B), "tile", 0, 0)
        return got.reshape(SLOTS, B)

    def vertical(s):
        up = [(i, (i + 1) % slabs) for i in range(slabs)]
        return lax.ppermute(s, "slab", up), lax.ppermute(s, "slab", [(j, i) for i, j in up])

    t, send = call(
        first_kernel, "first", (fetch_rows, root_count), (soil_pre, soil_rhs), (soil, (TILES, PIECE, B))
    )
    got = lax.all_to_all(send, "tile", 0, 0)
    s, send, choice, ur = call(
        first_step_kernel, "step0",
        (own_cols, margin_slot, fetch_rows, root_count),
        (soil_diag, soil_off, soil_pre, t, got, soil_rhs, root_pre, root_rhs),
        (soil, table, table, root), (pltpu.VMEM(soil, F32),),
    )
    x, r, rr, root_x = s, soil_rhs, root_rhs, ur
    rho = 1.0 / SIGMA
    for sweep in range(SWEEPS):
        below, above = vertical(s)
        got = exchange(send)
        scalars = (own_cols, margin_slot, vertical_col, root_cell)
        if sweep + 1 == SWEEPS:
            (r,) = call(
                last_kernel, "last", scalars,
                (soil_diag, soil_off, root_down, s, got, below, above, r, ur), (soil,),
            )
            break
        rho_new = 1.0 / (2.0 * SIGMA - rho)
        keep, gain = rho_new * rho, 2.0 * rho_new / DELTA
        rho = rho_new
        t, r, ur, rr, root_x, send = call(
            functools.partial(residual_kernel, keep, gain), f"residual{sweep}",
            scalars + (root_count,),
            (soil_diag, soil_off, soil_pre, root_diag, root_pre, root_up, root_down,
             s, got, below, above, r, ur, rr, root_x, choice),
            (soil, soil, root, root, root, table),
        )
        got = exchange(send)
        s, x, send = call(
            functools.partial(step_kernel, keep, gain), f"step{sweep + 1}",
            (own_cols, margin_slot),
            (soil_diag, soil_off, soil_pre, t, got, r, s, x, choice),
            (soil, soil, table), (pltpu.VMEM(soil, F32),),
        )
    return x, root_x, r


def solution(mesh):
    split = P(("slab", "tile"))
    return jax.shard_map(
        body, mesh=mesh, in_specs=(split,) * 15, out_specs=(split,) * 3, check_vma=False
    )
```

```python
import functools

import jax
import jax.numpy as jnp
from jax import lax
from jax.experimental import pallas as pl
from jax.experimental.pallas import tpu as pltpu
from jax.sharding import PartitionSpec as P

SWEEPS = 3
LOW_BOUND = 0.25
HIGH_BOUND = 2.0
THETA = (HIGH_BOUND + LOW_BOUND) / 2.0
DELTA = (HIGH_BOUND - LOW_BOUND) / 2.0
SIGMA = THETA / DELTA

B = 128
NBD = 32
RCAP = 8
TILES = 16
CAP = 2
SLOTS = TILES * CAP
PIECE = NBD + 8
F32 = jnp.float32
OWN, MARGIN, VERT, CELL = 0, 2 * NBD, 3 * NBD, 4 * NBD
ENTRIES = CELL + RCAP

VMEM = pl.BlockSpec(memory_space=pltpu.VMEM)
SMEM = pl.BlockSpec(memory_space=pltpu.SMEM)


def row_sum(acc):
    lane = lax.broadcasted_iota(jnp.int32, (8, B), 1)
    sub = lax.broadcasted_iota(jnp.int32, (8, B), 0)
    ahead = lane - sub
    sums = jnp.sum(acc.reshape(B // 8, 8, B), axis=2, keepdims=True)
    out = jnp.zeros((8, B), F32)
    for k in range(B // 8):
        out = jnp.where(ahead == 8 * k, sums[k], out)
    return jnp.sum(out, axis=0, keepdims=True)


def product(*pairs):
    acc = None
    for mat, vec in pairs:
        term = mat * vec
        acc = term if acc is None else acc + term
    return row_sum(acc)


def row(ref, index):
    return ref[pl.ds(index, 1), :]


def at(ref, g):
    return ref[g : g + 1, :]


def pick(choice, values):
    return jnp.dot(
        choice[:, :NBD], values, precision=lax.Precision.HIGHEST, preferred_element_type=F32
    )


def anchor_kernel(out):
    out[...] = jnp.zeros_like(out)


def first_kernel(count, anchor, fetch, pre, rhs, t_out, send):
    for g in range(NBD):
        t_out[g : g + 1, :] = product((pre[g], at(rhs, g)))
    t = t_out[...]
    asked = fetch[0].astype(F32)
    lane = lax.broadcasted_iota(jnp.int32, asked.shape, 1)
    for p in range(TILES):
        send[p, :NBD, :] = t
        mine = jnp.sum(jnp.where(lane == p, asked, 0.0), axis=1, keepdims=True)
        send[p, NBD : NBD + CAP, :] = jnp.broadcast_to(mine, (CAP, B))


def extended_rows(own, near_row, diag, off, pre, t, res, w):
    for g in range(NBD):
        w[g : g + 1, :] = at(res, g) - product(
            (diag[g], at(t, g)),
            (off[g, 0], row(t, own(0, g))),
            (off[g, 1], row(t, own(1, g))),
            (off[g, 2], near_row(g)),
        )


def first_step_kernel(
    own, margin, vert, cell, fetch, count, diag, off, pre, t, table, rhs, root_pre, root_rhs,
    s_out, send, choice, index, live, ur_out, w,
):
    def near_row(g):
        peer = margin[g] // CAP
        return table[peer, pl.ds(fetch[0, margin[g] % CAP, peer], 1), :]

    def note(entry, value):
        index[entry : entry + 1, :] = jnp.full((1, B), value, jnp.int32)

    for g in range(NBD):
        note(OWN + g, own[0, g])
        note(OWN + NBD + g, own[1, g])
        note(MARGIN + g, margin[g])
        note(VERT + g, vert[g])
    for r in range(RCAP):
        note(CELL + r, cell[r])
    extended_rows(lambda k, g: own[k, g], near_row, diag, off, pre, t, rhs, w)
    for g in range(NBD):
        z = at(t, g) + product((pre[g], at(w, g)))
        s_out[g : g + 1, :] = z * (1.0 / THETA)
    lane = lax.broadcasted_iota(jnp.int32, (CAP, B), 1).astype(F32)
    for p in range(TILES):
        choice[CAP * p : CAP * (p + 1), :] = (table[p, NBD : NBD + CAP, :] == lane).astype(F32)
    send[...] = pick(choice[...], s_out[...])
    slot = lax.broadcasted_iota(jnp.int32, (RCAP, B), 0)
    live[...] = (slot < count[0]).astype(F32)
    for r in range(RCAP):
        z = product((root_pre[r], at(root_rhs, r)))
        ur_out[r : r + 1, :] = jnp.where(at(live, r) > 0.0, z * (1.0 / THETA), 0.0)


def step_kernel(
    keep, gain, index, diag, off, pre, t, table, res, s_in, choice, s_out, send, w,
):
    def own(k, g):
        return index[OWN + k * NBD + g, 0]

    extended_rows(own, lambda g: row(table, index[MARGIN + g, 0]), diag, off, pre, t, res, w)
    for g in range(NBD):
        z = at(t, g) + product((pre[g], at(w, g)))
        s_out[g : g + 1, :] = keep * at(s_in, g) + gain * z
    send[...] = pick(choice[...], s_out[...])


def residual_rows(index, diag, off, down, s, table, below, above, res, ur, r_out):
    r_out[...] = res[...]
    for r in range(RCAP):
        spot = pl.ds(index[CELL + r, 0], 1)
        r_out[spot, :] = r_out[spot, :] - product((down[r], at(ur, r)))
    for g in range(NBD):
        vert = index[VERT + g, 0]
        over = jnp.where(vert < NBD, row(below, vert % NBD), row(above, vert % NBD))
        r_out[g : g + 1, :] = at(r_out, g) - product(
            (diag[g], at(s, g)),
            (off[g, 0], row(s, index[OWN + g, 0])),
            (off[g, 1], row(s, index[OWN + NBD + g, 0])),
            (off[g, 2], row(table, index[MARGIN + g, 0])),
            (off[g, 3], over),
        )


def residual_kernel(
    keep, gain, index, diag, off, pre, root_diag, root_pre, root_up, down,
    s, table, below, above, res, ur, rr, live, choice,
    t_out, r_out, ur_out, send, rr_out,
):
    residual_rows(index, diag, off, down, s, table, below, above, res, ur, r_out)
    for g in range(NBD):
        t_out[g : g + 1, :] = product((pre[g], at(r_out, g)))
    send[...] = pick(choice[...], t_out[...])
    for r in range(RCAP):
        change = product(
            (root_diag[r], at(ur, r)), (root_up[r], row(s, index[CELL + r, 0]))
        )
        rr_out[r : r + 1, :] = at(rr, r) - change
    for r in range(RCAP):
        z = product((root_pre[r], at(rr_out, r)))
        ur_out[r : r + 1, :] = jnp.where(
            at(live, r) > 0.0, keep * at(ur, r) + gain * z, 0.0
        )


def last_kernel(
    index, diag, off, down, s, table, below, above, res, ur, s_first, s_before, ur_first, ur_before,
    r_out, x_out, root_x,
):
    x_out[...] = s_first[...] + s_before[...] + s[...]
    root_x[...] = ur_first[...] + ur_before[...] + ur[...]
    residual_rows(index, diag, off, down, s, table, below, above, res, ur, r_out)


def call(kernel, name, scalars, arrays, outs, scratch=()):
    shapes = [s if isinstance(s, jax.ShapeDtypeStruct) else jax.ShapeDtypeStruct(s, F32) for s in outs]
    return pl.pallas_call(
        kernel,
        out_shape=tuple(shapes),
        in_specs=[SMEM] * len(scalars) + [VMEM] * len(arrays),
        out_specs=(VMEM,) * len(outs),
        scratch_shapes=[pltpu.VMEM(shape, F32) for shape in scratch],
        compiler_params=pltpu.CompilerParams(vmem_limit_bytes=4 * 2**20),
        cost_estimate=pl.CostEstimate(
            flops=20_000_000_000, transcendentals=0, bytes_accessed=40_000_000
        ),
        name=name,
    )(*scalars, *arrays)


def body(
    soil_diag, soil_off, soil_pre, own_cols, margin_slot, vertical_col, fetch_rows, soil_rhs,
    root_diag, root_pre, root_up, root_down, root_cell, root_count, root_rhs,
):
    slabs = lax.axis_size("slab")
    own_cols, fetch_rows = own_cols.T, jnp.swapaxes(fetch_rows, 1, 2)
    soil, root, table = (NBD, B), (RCAP, B), (SLOTS, B)

    def exchange(rows):
        got = lax.all_to_all(rows.reshape(TILES, CAP, B), "tile", 0, 0)
        return got.reshape(SLOTS, B)

    def vertical(s):
        up = [(i, (i + 1) % slabs) for i in range(slabs)]
        above = lax.ppermute(s, "slab", [(j, i) for i, j in up])
        return lax.ppermute(s, "slab", up), above

    (anchor,) = call(anchor_kernel, "anchor", (), (), (root,))
    t, send = call(
        first_kernel, "first", (root_count,), (anchor, fetch_rows, soil_pre, soil_rhs), (soil, (TILES, PIECE, B))
    )
    got = lax.all_to_all(send, "tile", 0, 0)
    s, send, choice, index, live, ur = call(
        first_step_kernel, "step0",
        (own_cols, margin_slot, vertical_col, root_cell, fetch_rows, root_count),
        (soil_diag, soil_off, soil_pre, t, got, soil_rhs, root_pre, root_rhs),
        (soil, table, table, jax.ShapeDtypeStruct((ENTRIES, B), jnp.int32), root, root),
        (soil,),
    )
    r, rr, steps, urs = soil_rhs, root_rhs, [s], [ur]
    rho = 1.0 / SIGMA
    for sweep in range(SWEEPS):
        below, above = vertical(s)
        got = exchange(send)
        if sweep + 1 == SWEEPS:
            r, x, root_x = call(
                last_kernel, "last", (),
                (index, soil_diag, soil_off, root_down, s, got, below, above, r, ur, *steps[:2], *urs[:2]),
                (soil, soil, root),
            )
            break
        rho_new = 1.0 / (2.0 * SIGMA - rho)
        keep, gain = rho_new * rho, 2.0 * rho_new / DELTA
        rho = rho_new
        more = sweep + 2 < SWEEPS
        t, r, ur, send, *rest = call(
            functools.partial(residual_kernel, keep, gain), f"residual{sweep}", (),
            (index, soil_diag, soil_off, soil_pre, root_diag, root_pre, root_up, root_down,
             s, got, below, above, r, urs[-1], rr, live, choice),
            (soil, soil, root, table) + (root,) * more, (root,) * (not more),
        )
        rr = rest[0] if more else None
        urs.append(ur)
        got = exchange(send)
        s, send = call(
            functools.partial(step_kernel, keep, gain), f"step{sweep + 1}", (),
            (index, soil_diag, soil_off, soil_pre, t, got, r, s, choice),
            (soil, table), (soil,),
        )
        steps.append(s)
    return x, root_x, r


def solution(mesh):
    split = P(("slab", "tile"))
    return jax.shard_map(
        body, mesh=mesh, in_specs=(split,) * 15, out_specs=(split,) * 3, check_vma=False
    )
```

```python
import functools

import jax
import jax.numpy as jnp
from jax import lax
from jax.experimental import pallas as pl
from jax.experimental.pallas import tpu as pltpu
from jax.sharding import PartitionSpec as P

SWEEPS = 3
LOW_BOUND = 0.25
HIGH_BOUND = 2.0
THETA = (HIGH_BOUND + LOW_BOUND) / 2.0
DELTA = (HIGH_BOUND - LOW_BOUND) / 2.0
SIGMA = THETA / DELTA

B = 128
NBD = 32
RCAP = 8
TILES = 16
CAP = 2
SLOTS = TILES * CAP
PIECE = NBD + 8
F32 = jnp.float32
OWN, MARGIN, VERT, WIDE, CELL = 0, 2 * NBD, 3 * NBD, 4 * NBD, 5 * NBD
ENTRIES = CELL + RCAP
LAG = 6

VMEM = pl.BlockSpec(memory_space=pltpu.VMEM)
SMEM = pl.BlockSpec(memory_space=pltpu.SMEM)


def row_sum(acc):
    lane = lax.broadcasted_iota(jnp.int32, (8, B), 1)
    sub = lax.broadcasted_iota(jnp.int32, (8, B), 0)
    ahead = lane - sub
    sums = jnp.sum(acc.reshape(B // 8, 8, B), axis=2, keepdims=True)
    out = jnp.zeros((8, B), F32)
    for k in range(B // 8):
        out = jnp.where(ahead == 8 * k, sums[k], out)
    return jnp.sum(out, axis=0, keepdims=True)


def product(*pairs):
    acc = None
    for mat, vec in pairs:
        term = mat * vec
        acc = term if acc is None else acc + term
    return row_sum(acc)


def row(ref, index):
    return ref[pl.ds(index, 1), :]


def at(ref, g):
    return ref[g : g + 1, :]


def send_rows(asked, values, send):
    for q in range(SLOTS):
        send[q : q + 1, :] = row(values, asked[q, 0])


def anchor_kernel(out):
    out[...] = jnp.zeros_like(out)


def list_kernel(own, margin, vert, cell, fetch, count, anchor, index, wish, live):
    def note(entry, value):
        index[entry : entry + 1, :] = jnp.full((1, B), value, jnp.int32)

    for g in range(NBD):
        note(OWN + g, own[0, g])
        note(OWN + NBD + g, own[1, g])
        note(MARGIN + g, margin[g])
        note(VERT + g, vert[g])
        peer = margin[g] // CAP
        note(WIDE + g, peer * PIECE + fetch[0, margin[g] % CAP, peer])
    for r in range(RCAP):
        note(CELL + r, cell[r])
    for q in range(SLOTS):
        wish[q : q + 1, :] = jnp.full((1, B), fetch[0, q % CAP, q // CAP], jnp.int32).astype(F32)
    slot = lax.broadcasted_iota(jnp.int32, (RCAP, B), 0)
    live[...] = (slot < count[0]).astype(F32)


def first_kernel(wish, pre, rhs, t_out, send):
    for g in range(NBD):
        t_out[g : g + 1, :] = product((pre[g], at(rhs, g)))
    t = t_out[...]
    for p in range(TILES):
        send[p, :NBD, :] = t
        send[p, NBD : NBD + CAP, :] = wish[CAP * p : CAP * (p + 1), :]


def staggered(first, second):
    for g in range(NBD + LAG):
        if g < NBD:
            first(g)
        if g >= LAG:
            second(g - LAG)


def step_rows(index, near, near_at, diag, off, pre, t, res, w, finish):
    def extended(g):
        w[g : g + 1, :] = at(res, g) - product(
            (diag[g], at(t, g)),
            (off[g, 0], row(t, index[OWN + g, 0])),
            (off[g, 1], row(t, index[OWN + NBD + g, 0])),
            (off[g, 2], row(near, index[near_at + g, 0])),
        )

    def turn(g):
        finish(g, at(t, g) + product((pre[g], at(w, g))))

    staggered(extended, turn)


def first_step_kernel(
    index, live, diag, off, pre, t, table, rhs, root_pre, root_rhs,
    s_out, send, asked, ur_out, w,
):
    for p in range(TILES):
        asked[CAP * p : CAP * (p + 1), :] = table[
            PIECE * p + NBD : PIECE * p + NBD + CAP, :
        ].astype(jnp.int32)

    def finish(g, z):
        s_out[g : g + 1, :] = z * (1.0 / THETA)

    step_rows(index, table, WIDE, diag, off, pre, t, rhs, w, finish)
    for r in range(RCAP):
        z = product((root_pre[r], at(root_rhs, r)))
        ur_out[r : r + 1, :] = jnp.where(at(live, r) > 0.0, z * (1.0 / THETA), 0.0)
    send_rows(asked, s_out, send)


def step_kernel(keep, gain, index, diag, off, pre, t, table, res, s_in, asked, s_out, send, w):
    def finish(g, z):
        s_out[g : g + 1, :] = keep * at(s_in, g) + gain * z

    step_rows(index, table, MARGIN, diag, off, pre, t, res, w, finish)
    send_rows(asked, s_out, send)


def residual_rows(index, diag, off, down, s, table, below, above, res, ur, r_out, after=None):
    r_out[...] = res[...]
    for r in range(RCAP):
        spot = pl.ds(index[CELL + r, 0], 1)
        r_out[spot, :] = r_out[spot, :] - product((down[r], at(ur, r)))

    def applied(g):
        vert = index[VERT + g, 0]
        over = jnp.where(vert < NBD, row(below, vert % NBD), row(above, vert % NBD))
        r_out[g : g + 1, :] = at(r_out, g) - product(
            (diag[g], at(s, g)),
            (off[g, 0], row(s, index[OWN + g, 0])),
            (off[g, 1], row(s, index[OWN + NBD + g, 0])),
            (off[g, 2], row(table, index[MARGIN + g, 0])),
            (off[g, 3], over),
        )

    staggered(applied, after or (lambda g: None))


def residual_kernel(
    keep, gain, index, diag, off, pre, root_diag, root_pre, root_up, down,
    s, table, below, above, res, ur, rr, live, asked,
    t_out, r_out, ur_out, send, rr_out,
):
    for r in range(RCAP):
        change = product(
            (root_diag[r], at(ur, r)), (root_up[r], row(s, index[CELL + r, 0]))
        )
        rr_out[r : r + 1, :] = at(rr, r) - change

    def turn(g):
        t_out[g : g + 1, :] = product((pre[g], at(r_out, g)))

    residual_rows(index, diag, off, down, s, table, below, above, res, ur, r_out, turn)
    for r in range(RCAP):
        z = product((root_pre[r], at(rr_out, r)))
        ur_out[r : r + 1, :] = jnp.where(
            at(live, r) > 0.0, keep * at(ur, r) + gain * z, 0.0
        )
    send_rows(asked, t_out, send)


def last_kernel(
    index, diag, off, down, s, table, below, above, res, ur, s_first, s_before, ur_first, ur_before,
    r_out, x_out, root_x,
):
    x_out[...] = s_first[...] + s_before[...] + s[...]
    root_x[...] = ur_first[...] + ur_before[...] + ur[...]
    residual_rows(index, diag, off, down, s, table, below, above, res, ur, r_out)


def call(kernel, name, scalars, arrays, outs, scratch=(), work=20_000_000_000):
    shapes = [s if isinstance(s, jax.ShapeDtypeStruct) else jax.ShapeDtypeStruct(s, F32) for s in outs]
    return pl.pallas_call(
        kernel,
        out_shape=tuple(shapes),
        in_specs=[SMEM] * len(scalars) + [VMEM] * len(arrays),
        out_specs=(VMEM,) * len(outs),
        scratch_shapes=[pltpu.VMEM(shape, F32) for shape in scratch],
        compiler_params=pltpu.CompilerParams(vmem_limit_bytes=4 * 2**20),
        cost_estimate=pl.CostEstimate(
            flops=work, transcendentals=0, bytes_accessed=work // 500
        ),
        name=name,
    )(*scalars, *arrays)


def body(
    soil_diag, soil_off, soil_pre, own_cols, margin_slot, vertical_col, fetch_rows, soil_rhs,
    root_diag, root_pre, root_up, root_down, root_cell, root_count, root_rhs,
):
    slabs = lax.axis_size("slab")
    own_cols, fetch_rows = own_cols.T, jnp.swapaxes(fetch_rows, 1, 2)
    soil, root, table = (NBD, B), (RCAP, B), (SLOTS, B)

    def exchange(rows):
        got = lax.all_to_all(rows.reshape(TILES, CAP, B), "tile", 0, 0)
        return got.reshape(SLOTS, B)

    def vertical(s):
        up = [(i, (i + 1) % slabs) for i in range(slabs)]
        above = lax.ppermute(s, "slab", [(j, i) for i, j in up])
        return lax.ppermute(s, "slab", up), above

    (anchor,) = call(anchor_kernel, "anchor", (), (), (root,))
    entries = jax.ShapeDtypeStruct((ENTRIES, B), jnp.int32)
    index, wish, live = call(
        list_kernel, "lists",
        (own_cols, margin_slot, vertical_col, root_cell, fetch_rows, root_count),
        (anchor,), (entries, table, root), work=1000,
    )
    t, send = call(
        first_kernel, "first", (), (wish, soil_pre, soil_rhs), (soil, (TILES, PIECE, B))
    )
    got = lax.all_to_all(send, "tile", 0, 0).reshape(TILES * PIECE, B)
    s, send, asked, ur = call(
        first_step_kernel, "step0", (),
        (index, live, soil_diag, soil_off, soil_pre, t, got, soil_rhs, root_pre, root_rhs),
        (soil, table, jax.ShapeDtypeStruct(table, jnp.int32), root), (soil,),
    )
    r, rr, steps, urs = soil_rhs, root_rhs, [s], [ur]
    rho = 1.0 / SIGMA
    for sweep in range(SWEEPS):
        below, above = vertical(s)
        got = exchange(send)
        if sweep + 1 == SWEEPS:
            r, x, root_x = call(
                last_kernel, "last", (),
                (index, soil_diag, soil_off, root_down, s, got, below, above, r, ur, *steps[:2], *urs[:2]),
                (soil, soil, root),
            )
            break
        rho_new = 1.0 / (2.0 * SIGMA - rho)
        keep, gain = rho_new * rho, 2.0 * rho_new / DELTA
        rho = rho_new
        more = sweep + 2 < SWEEPS
        t, r, ur, send, *rest = call(
            functools.partial(residual_kernel, keep, gain), f"residual{sweep}", (),
            (index, soil_diag, soil_off, soil_pre, root_diag, root_pre, root_up, root_down,
             s, got, below, above, r, urs[-1], rr, live, asked),
            (soil, soil, root, table) + (root,) * more, (root,) * (not more),
        )
        rr = rest[0] if more else None
        urs.append(ur)
        got = exchange(send)
        s, send = call(
            functools.partial(step_kernel, keep, gain), f"step{sweep + 1}", (),
            (index, soil_diag, soil_off, soil_pre, t, got, r, s, asked),
            (soil, table), (soil,),
        )
        steps.append(s)
    return x, root_x, r


def solution(mesh):
    split = P(("slab", "tile"))
    return jax.shard_map(
        body, mesh=mesh, in_specs=(split,) * 15, out_specs=(split,) * 3, check_vma=False
    )
```

```python
import functools

import jax
import jax.numpy as jnp
from jax import lax
from jax.experimental import pallas as pl
from jax.experimental.pallas import tpu as pltpu
from jax.sharding import PartitionSpec as P

SWEEPS = 3
LOW_BOUND = 0.25
HIGH_BOUND = 2.0
THETA = (HIGH_BOUND + LOW_BOUND) / 2.0
DELTA = (HIGH_BOUND - LOW_BOUND) / 2.0
SIGMA = THETA / DELTA

B = 128
NBD = 32
RCAP = 8
TILES = 16
CAP = 2
SLOTS = TILES * CAP
PIECE = NBD + CAP
F32 = jnp.float32
OWN, MARGIN, VERT, WIDE, CELL = 0, 2 * NBD, 3 * NBD, 4 * NBD, 5 * NBD
ENTRIES = CELL + RCAP
LAG = 8

VMEM = pl.BlockSpec(memory_space=pltpu.VMEM)
SMEM = pl.BlockSpec(memory_space=pltpu.SMEM)


def row_sum(acc):
    lane = lax.broadcasted_iota(jnp.int32, (8, B), 1)
    sub = lax.broadcasted_iota(jnp.int32, (8, B), 0)
    ahead = lane - sub
    sums = jnp.sum(acc.reshape(B // 8, 8, B), axis=2, keepdims=True)
    out = jnp.zeros((8, B), F32)
    for k in range(B // 8):
        out = jnp.where(ahead == 8 * k, sums[k], out)
    return jnp.sum(out, axis=0, keepdims=True)


def product(*pairs):
    acc = None
    for mat, vec in pairs:
        term = mat * vec
        acc = term if acc is None else acc + term
    return row_sum(acc)


def row(ref, index):
    return ref[pl.ds(index, 1), :]


def at(ref, g):
    return ref[g : g + 1, :]


def send_rows(asked, values, send):
    for q in range(SLOTS):
        send[q : q + 1, :] = row(values, asked[q, 0])


def anchor_kernel(out):
    out[...] = jnp.zeros_like(out)


def list_kernel(own, margin, vert, cell, fetch, count, anchor, index, wish, live):
    def note(entry, value):
        index[entry : entry + 1, :] = jnp.full((1, B), value, jnp.int32)

    for g in range(NBD):
        note(OWN + g, own[0, g])
        note(OWN + NBD + g, own[1, g])
        note(MARGIN + g, margin[g])
        note(VERT + g, vert[g])
        peer = margin[g] // CAP
        note(WIDE + g, peer * PIECE + fetch[0, margin[g] % CAP, peer])
    for r in range(RCAP):
        note(CELL + r, cell[r])
    for q in range(SLOTS):
        wish[q : q + 1, :] = jnp.full((1, B), fetch[0, q % CAP, q // CAP], jnp.int32).astype(F32)
    slot = lax.broadcasted_iota(jnp.int32, (RCAP, B), 0)
    live[...] = (slot < count[0]).astype(F32)


def first_kernel(wish, pre, rhs, t_out, send):
    for g in range(NBD):
        t_out[g : g + 1, :] = product((pre[g], at(rhs, g)))
    t = t_out[...]
    for p in range(TILES):
        send[PIECE * p : PIECE * p + NBD, :] = t
        send[PIECE * p + NBD : PIECE * (p + 1), :] = wish[CAP * p : CAP * (p + 1), :]


def staggered(first, second):
    for g in range(NBD + LAG):
        if g < NBD:
            first(g)
        if g >= LAG:
            second(g - LAG)


def step_rows(index, near, near_at, diag, off, pre, t, res, w, finish):
    def extended(g):
        w[g : g + 1, :] = at(res, g) - product(
            (diag[g], at(t, g)),
            (off[g, 0], row(t, index[OWN + g, 0])),
            (off[g, 1], row(t, index[OWN + NBD + g, 0])),
            (off[g, 2], row(near, index[near_at + g, 0])),
        )

    def turn(g):
        finish(g, at(t, g) + product((pre[g], at(w, g))))

    staggered(extended, turn)


def first_step_kernel(
    index, live, diag, off, pre, t, table, rhs, root_pre, root_rhs,
    s_out, send, asked, ur_out, w,
):
    for p in range(TILES):
        asked[CAP * p : CAP * (p + 1), :] = table[
            PIECE * p + NBD : PIECE * p + NBD + CAP, :
        ].astype(jnp.int32)

    def finish(g, z):
        s_out[g : g + 1, :] = z * (1.0 / THETA)

    step_rows(index, table, WIDE, diag, off, pre, t, rhs, w, finish)
    for r in range(RCAP):
        z = product((root_pre[r], at(root_rhs, r)))
        ur_out[r : r + 1, :] = jnp.where(at(live, r) > 0.0, z * (1.0 / THETA), 0.0)
    send_rows(asked, s_out, send)


def step_kernel(keep, gain, index, diag, off, pre, t, table, res, s_in, asked, s_out, send, w):
    def finish(g, z):
        s_out[g : g + 1, :] = keep * at(s_in, g) + gain * z

    step_rows(index, table, MARGIN, diag, off, pre, t, res, w, finish)
    send_rows(asked, s_out, send)


def residual_rows(index, diag, off, down, s, table, below, above, res, ur, r_out, after=None):
    r_out[...] = res[...]
    for r in range(RCAP):
        spot = pl.ds(index[CELL + r, 0], 1)
        r_out[spot, :] = r_out[spot, :] - product((down[r], at(ur, r)))

    def applied(g):
        vert = index[VERT + g, 0]
        over = jnp.where(vert < NBD, row(below, vert % NBD), row(above, vert % NBD))
        r_out[g : g + 1, :] = at(r_out, g) - product(
            (diag[g], at(s, g)),
            (off[g, 0], row(s, index[OWN + g, 0])),
            (off[g, 1], row(s, index[OWN + NBD + g, 0])),
            (off[g, 2], row(table, index[MARGIN + g, 0])),
            (off[g, 3], over),
        )

    staggered(applied, after or (lambda g: None))


def residual_kernel(
    keep, gain, index, diag, off, pre, root_diag, root_pre, root_up, down,
    s, table, below, above, res, ur, rr, live, asked,
    t_out, r_out, ur_out, send, rr_out,
):
    for r in range(RCAP):
        change = product(
            (root_diag[r], at(ur, r)), (root_up[r], row(s, index[CELL + r, 0]))
        )
        rr_out[r : r + 1, :] = at(rr, r) - change

    def turn(g):
        t_out[g : g + 1, :] = product((pre[g], at(r_out, g)))

    residual_rows(index, diag, off, down, s, table, below, above, res, ur, r_out, turn)
    for r in range(RCAP):
        z = product((root_pre[r], at(rr_out, r)))
        ur_out[r : r + 1, :] = jnp.where(
            at(live, r) > 0.0, keep * at(ur, r) + gain * z, 0.0
        )
    send_rows(asked, t_out, send)


def last_kernel(
    index, diag, off, down, s, table, below, above, res, ur, s_first, s_before, ur_first, ur_before,
    r_out, x_out, root_x,
):
    x_out[...] = s_first[...] + s_before[...] + s[...]
    root_x[...] = ur_first[...] + ur_before[...] + ur[...]
    residual_rows(index, diag, off, down, s, table, below, above, res, ur, r_out)


def call(kernel, name, scalars, arrays, outs, scratch=(), work=20_000_000_000):
    shapes = [s if isinstance(s, jax.ShapeDtypeStruct) else jax.ShapeDtypeStruct(s, F32) for s in outs]
    return pl.pallas_call(
        kernel,
        out_shape=tuple(shapes),
        in_specs=[SMEM] * len(scalars) + [VMEM] * len(arrays),
        out_specs=(VMEM,) * len(outs),
        scratch_shapes=[pltpu.VMEM(shape, F32) for shape in scratch],
        compiler_params=pltpu.CompilerParams(vmem_limit_bytes=4 * 2**20),
        cost_estimate=pl.CostEstimate(
            flops=work, transcendentals=0, bytes_accessed=work // 500
        ),
        name=name,
    )(*scalars, *arrays)


def body(
    soil_diag, soil_off, soil_pre, own_cols, margin_slot, vertical_col, fetch_rows, soil_rhs,
    root_diag, root_pre, root_up, root_down, root_cell, root_count, root_rhs,
):
    slabs = lax.axis_size("slab")
    own_cols, fetch_rows = own_cols.T, jnp.swapaxes(fetch_rows, 1, 2)
    soil, root, table = (NBD, B), (RCAP, B), (SLOTS, B)

    def exchange(rows):
        pieces = rows.reshape(TILES, -1, CAP, B)
        return lax.all_to_all(pieces, "tile", 0, 0).reshape(rows.shape)

    def vertical(s):
        up = [(i, (i + 1) % slabs) for i in range(slabs)]
        above = lax.ppermute(s, "slab", [(j, i) for i, j in up])
        return lax.ppermute(s, "slab", up), above

    (anchor,) = call(anchor_kernel, "anchor", (), (), (root,))
    entries = jax.ShapeDtypeStruct((ENTRIES, B), jnp.int32)
    index, wish, live = call(
        list_kernel, "lists",
        (own_cols, margin_slot, vertical_col, root_cell, fetch_rows, root_count),
        (anchor,), (entries, table, root), work=1000,
    )
    t, send = call(
        first_kernel, "first", (), (wish, soil_pre, soil_rhs), (soil, (TILES * PIECE, B))
    )
    got = exchange(send)
    s, send, asked, ur = call(
        first_step_kernel, "step0", (),
        (index, live, soil_diag, soil_off, soil_pre, t, got, soil_rhs, root_pre, root_rhs),
        (soil, table, jax.ShapeDtypeStruct(table, jnp.int32), root), (soil,),
    )
    r, rr, steps, urs = soil_rhs, root_rhs, [s], [ur]
    rho = 1.0 / SIGMA
    for sweep in range(SWEEPS):
        below, above = vertical(s)
        got = exchange(send)
        if sweep + 1 == SWEEPS:
            r, x, root_x = call(
                last_kernel, "last", (),
                (index, soil_diag, soil_off, root_down, s, got, below, above, r, ur, *steps[:2], *urs[:2]),
                (soil, soil, root),
            )
            break
        rho_new = 1.0 / (2.0 * SIGMA - rho)
        keep, gain = rho_new * rho, 2.0 * rho_new / DELTA
        rho = rho_new
        more = sweep + 2 < SWEEPS
        t, r, ur, send, *rest = call(
            functools.partial(residual_kernel, keep, gain), f"residual{sweep}", (),
            (index, soil_diag, soil_off, soil_pre, root_diag, root_pre, root_up, root_down,
             s, got, below, above, r, urs[-1], rr, live, asked),
            (soil, soil, root, table) + (root,) * more, (root,) * (not more),
        )
        rr = rest[0] if more else None
        urs.append(ur)
        got = exchange(send)
        s, send = call(
            functools.partial(step_kernel, keep, gain), f"step{sweep + 1}", (),
            (index, soil_diag, soil_off, soil_pre, t, got, r, s, asked),
            (soil, table), (soil,),
        )
        steps.append(s)
    return x, root_x, r


def solution(mesh):
    split = P(("slab", "tile"))
    return jax.shard_map(
        body, mesh=mesh, in_specs=(split,) * 15, out_specs=(split,) * 3, check_vma=False
    )
```

```python
import functools

import jax
import jax.numpy as jnp
from jax import lax
from jax.experimental import pallas as pl
from jax.experimental.pallas import tpu as pltpu
from jax.sharding import PartitionSpec as P

SWEEPS = 3
LOW_BOUND = 0.25
HIGH_BOUND = 2.0
THETA = (HIGH_BOUND + LOW_BOUND) / 2.0
DELTA = (HIGH_BOUND - LOW_BOUND) / 2.0
SIGMA = THETA / DELTA

B = 128
NBD = 32
RCAP = 8
TILES = 16
CAP = 2
SLOTS = TILES * CAP
PIECE = NBD + CAP
F32 = jnp.float32
OWN, MARGIN, VERT, WIDE, CELL = 0, 2 * NBD, 3 * NBD, 4 * NBD, 5 * NBD
ENTRIES = CELL + RCAP
LAG = 8
AHEAD = 4

VMEM = pl.BlockSpec(memory_space=pltpu.VMEM)
SMEM = pl.BlockSpec(memory_space=pltpu.SMEM)


def diagonal(rows):
    lane = lax.broadcasted_iota(jnp.int32, (8, B), 1)
    sub = lax.broadcasted_iota(jnp.int32, (8, B), 0)
    bit = 8
    while len(rows) > 1:
        high = (lane & bit) != 0
        rows = [jnp.where(high, b, a) for a, b in zip(rows[::2], rows[1::2])]
        bit *= 2
    return jnp.sum(jnp.where((lane & 7) == sub, rows[0], 0.0), axis=0, keepdims=True)


def lane_sums(acc):
    sums = jnp.sum(acc.reshape(B // 8, 8, B), axis=2, keepdims=True)
    return diagonal([jnp.broadcast_to(sums[k], (8, B)) for k in range(B // 8)])


def matrix_sums(acc):
    high = acc.astype(jnp.bfloat16)
    low = (acc - high.astype(F32)).astype(jnp.bfloat16)
    sums = jnp.dot(
        jnp.concatenate([high, low], axis=1),
        jnp.ones((2 * B, B), jnp.bfloat16),
        preferred_element_type=F32,
    )
    return diagonal([sums[8 * k : 8 * k + 8] for k in range(B // 8)])


def product(*pairs, sums=lane_sums):
    acc = None
    for mat, vec in pairs:
        term = mat * vec
        acc = term if acc is None else acc + term
    return sums(acc)


def row(ref, index):
    return ref[pl.ds(index, 1), :]


def at(ref, g):
    return ref[g : g + 1, :]


def send_rows(asked, values, send):
    for q in range(SLOTS):
        send[q : q + 1, :] = row(values, asked[q, 0])


def anchor_kernel(out):
    out[...] = jnp.zeros_like(out)


def list_kernel(own, margin, vert, cell, fetch, count, anchor, index, wish, live):
    def note(entry, value):
        index[entry : entry + 1, :] = jnp.full((1, B), value, jnp.int32)

    for g in range(NBD):
        note(OWN + g, own[0, g])
        note(OWN + NBD + g, own[1, g])
        note(MARGIN + g, margin[g])
        note(VERT + g, vert[g])
        peer = margin[g] // CAP
        note(WIDE + g, peer * PIECE + fetch[0, margin[g] % CAP, peer])
    for r in range(RCAP):
        note(CELL + r, cell[r])
    for q in range(SLOTS):
        wish[q : q + 1, :] = jnp.full((1, B), fetch[0, q % CAP, q // CAP], jnp.int32).astype(F32)
    slot = lax.broadcasted_iota(jnp.int32, (RCAP, B), 0)
    live[...] = (slot < count[0]).astype(F32)


def first_kernel(wish, pre, rhs, t_out, send):
    for g in range(NBD):
        t_out[g : g + 1, :] = product(
            (pre[g], at(rhs, g)), sums=matrix_sums if g % 2 else lane_sums
        )
    t = t_out[...]
    for p in range(TILES):
        send[PIECE * p : PIECE * p + NBD, :] = t
        send[PIECE * p + NBD : PIECE * (p + 1), :] = wish[CAP * p : CAP * (p + 1), :]


def staggered(fetch_row, first, second):
    held = {}
    for g in range(-AHEAD, NBD + LAG):
        if g + AHEAD < NBD:
            held[g + AHEAD] = fetch_row(g + AHEAD)
        if 0 <= g < NBD:
            first(g, held.pop(g))
        if g >= LAG:
            second(g - LAG)


def step_rows(index, near, near_at, diag, off, pre, t, res, w, finish):
    def rows_of(g):
        return index[OWN + g, 0], index[OWN + NBD + g, 0], index[near_at + g, 0]

    def extended(g, at_rows):
        w[g : g + 1, :] = at(res, g) - product(
            (diag[g], at(t, g)),
            (off[g, 0], row(t, at_rows[0])),
            (off[g, 1], row(t, at_rows[1])),
            (off[g, 2], row(near, at_rows[2])),
        )

    def turn(g):
        finish(g, at(t, g) + product((pre[g], at(w, g))))

    staggered(rows_of, extended, turn)


def first_step_kernel(
    index, live, diag, off, pre, t, table, rhs, root_pre, root_rhs,
    s_out, send, asked, ur_out, w,
):
    for p in range(TILES):
        asked[CAP * p : CAP * (p + 1), :] = table[
            PIECE * p + NBD : PIECE * p + NBD + CAP, :
        ].astype(jnp.int32)

    def finish(g, z):
        s_out[g : g + 1, :] = z * (1.0 / THETA)

    step_rows(index, table, WIDE, diag, off, pre, t, rhs, w, finish)
    for r in range(RCAP):
        z = product((root_pre[r], at(root_rhs, r)), sums=matrix_sums)
        ur_out[r : r + 1, :] = jnp.where(at(live, r) > 0.0, z * (1.0 / THETA), 0.0)
    send_rows(asked, s_out, send)


def step_kernel(keep, gain, index, diag, off, pre, t, table, res, s_in, asked, s_out, send, w):
    def finish(g, z):
        s_out[g : g + 1, :] = keep * at(s_in, g) + gain * z

    step_rows(index, table, MARGIN, diag, off, pre, t, res, w, finish)
    send_rows(asked, s_out, send)


def residual_rows(index, diag, off, down, s, table, below, above, res, ur, r_out, after=None):
    r_out[...] = res[...]
    for r in range(RCAP):
        spot = pl.ds(index[CELL + r, 0], 1)
        r_out[spot, :] = r_out[spot, :] - product((down[r], at(ur, r)), sums=matrix_sums if after else lane_sums)

    def rows_of(g):
        return (
            index[OWN + g, 0], index[OWN + NBD + g, 0], index[MARGIN + g, 0], index[VERT + g, 0]
        )

    def applied(g, at_rows):
        vert = at_rows[3]
        over = jnp.where(vert < NBD, row(below, vert % NBD), row(above, vert % NBD))
        r_out[g : g + 1, :] = at(r_out, g) - product(
            (diag[g], at(s, g)),
            (off[g, 0], row(s, at_rows[0])),
            (off[g, 1], row(s, at_rows[1])),
            (off[g, 2], row(table, at_rows[2])),
            (off[g, 3], over),
        )

    staggered(rows_of, applied, after or (lambda g: None))


def residual_kernel(
    keep, gain, index, diag, off, pre, root_diag, root_pre, root_up, down,
    s, table, below, above, res, ur, rr, live, asked,
    t_out, r_out, ur_out, send, rr_out,
):
    def change_root(r):
        change = product(
            (root_diag[r], at(ur, r)), (root_up[r], row(s, index[CELL + r, 0])),
            sums=matrix_sums,
        )
        rr_out[r : r + 1, :] = at(rr, r) - change

    def turn_root(r):
        z = product((root_pre[r], at(rr_out, r)), sums=matrix_sums)
        ur_out[r : r + 1, :] = jnp.where(
            at(live, r) > 0.0, keep * at(ur, r) + gain * z, 0.0
        )

    def turn(g):
        t_out[g : g + 1, :] = product((pre[g], at(r_out, g)))
        if g % 2 == 0 and g < 2 * RCAP:
            change_root(g // 2)
        if g % 2 == 0 and g >= 2 * RCAP:
            turn_root(g // 2 - RCAP)

    residual_rows(index, diag, off, down, s, table, below, above, res, ur, r_out, turn)
    send_rows(asked, t_out, send)


def last_kernel(
    index, diag, off, down, s, table, below, above, res, ur, s_first, s_before, ur_first, ur_before,
    r_out, x_out, root_x,
):
    x_out[...] = s_first[...] + s_before[...] + s[...]
    root_x[...] = ur_first[...] + ur_before[...] + ur[...]
    residual_rows(index, diag, off, down, s, table, below, above, res, ur, r_out)


def call(kernel, name, scalars, arrays, outs, scratch=(), work=20_000_000_000):
    shapes = [s if isinstance(s, jax.ShapeDtypeStruct) else jax.ShapeDtypeStruct(s, F32) for s in outs]
    return pl.pallas_call(
        kernel,
        out_shape=tuple(shapes),
        in_specs=[SMEM] * len(scalars) + [VMEM] * len(arrays),
        out_specs=(VMEM,) * len(outs),
        scratch_shapes=[pltpu.VMEM(shape, F32) for shape in scratch],
        compiler_params=pltpu.CompilerParams(vmem_limit_bytes=4 * 2**20),
        cost_estimate=pl.CostEstimate(
            flops=work, transcendentals=0, bytes_accessed=work // 500
        ),
        name=name,
    )(*scalars, *arrays)


def body(
    soil_diag, soil_off, soil_pre, own_cols, margin_slot, vertical_col, fetch_rows, soil_rhs,
    root_diag, root_pre, root_up, root_down, root_cell, root_count, root_rhs,
):
    slabs = lax.axis_size("slab")
    own_cols, fetch_rows = own_cols.T, jnp.swapaxes(fetch_rows, 1, 2)
    soil, root, table = (NBD, B), (RCAP, B), (SLOTS, B)

    def exchange(rows):
        pieces = rows.reshape(TILES, -1, CAP, B)
        return lax.all_to_all(pieces, "tile", 0, 0).reshape(rows.shape)

    def vertical(s):
        up = [(i, (i + 1) % slabs) for i in range(slabs)]
        above = lax.ppermute(s, "slab", [(j, i) for i, j in up])
        return lax.ppermute(s, "slab", up), above

    (anchor,) = call(anchor_kernel, "anchor", (), (), (root,))
    entries = jax.ShapeDtypeStruct((ENTRIES, B), jnp.int32)
    index, wish, live = call(
        list_kernel, "lists",
        (own_cols, margin_slot, vertical_col, root_cell, fetch_rows, root_count),
        (anchor,), (entries, table, root), work=1000,
    )
    t, send = call(
        first_kernel, "first", (), (wish, soil_pre, soil_rhs), (soil, (TILES * PIECE, B))
    )
    got = exchange(send)
    s, send, asked, ur = call(
        first_step_kernel, "step0", (),
        (index, live, soil_diag, soil_off, soil_pre, t, got, soil_rhs, root_pre, root_rhs),
        (soil, table, jax.ShapeDtypeStruct(table, jnp.int32), root), (soil,),
    )
    r, rr, steps, urs = soil_rhs, root_rhs, [s], [ur]
    rho = 1.0 / SIGMA
    for sweep in range(SWEEPS):
        below, above = vertical(s)
        got = exchange(send)
        if sweep + 1 == SWEEPS:
            r, x, root_x = call(
                last_kernel, "last", (),
                (index, soil_diag, soil_off, root_down, s, got, below, above, r, ur, *steps[:2], *urs[:2]),
                (soil, soil, root),
            )
            break
        rho_new = 1.0 / (2.0 * SIGMA - rho)
        keep, gain = rho_new * rho, 2.0 * rho_new / DELTA
        rho = rho_new
        more = sweep + 2 < SWEEPS
        t, r, ur, send, *rest = call(
            functools.partial(residual_kernel, keep, gain), f"residual{sweep}", (),
            (index, soil_diag, soil_off, soil_pre, root_diag, root_pre, root_up, root_down,
             s, got, below, above, r, urs[-1], rr, live, asked),
            (soil, soil, root, table) + (root,) * more, (root,) * (not more),
        )
        rr = rest[0] if more else None
        urs.append(ur)
        got = exchange(send)
        s, send = call(
            functools.partial(step_kernel, keep, gain), f"step{sweep + 1}", (),
            (index, soil_diag, soil_off, soil_pre, t, got, r, s, asked),
            (soil, table), (soil,),
        )
        steps.append(s)
    return x, root_x, r


def solution(mesh):
    split = P(("slab", "tile"))
    return jax.shard_map(
        body, mesh=mesh, in_specs=(split,) * 15, out_specs=(split,) * 3, check_vma=False
    )
```

```python
import functools

import jax
import jax.numpy as jnp
from jax import lax
from jax.experimental import pallas as pl
from jax.experimental.pallas import tpu as pltpu
from jax.sharding import PartitionSpec as P

SWEEPS = 3
LOW_BOUND = 0.25
HIGH_BOUND = 2.0
THETA = (HIGH_BOUND + LOW_BOUND) / 2.0
DELTA = (HIGH_BOUND - LOW_BOUND) / 2.0
SIGMA = THETA / DELTA

B = 128
NBD = 32
RCAP = 8
TILES = 16
CAP = 2
SLOTS = TILES * CAP
PIECE = NBD + CAP
F32 = jnp.float32
OWN, MARGIN, VERT, WIDE, CELL = 0, 2 * NBD, 3 * NBD, 4 * NBD, 5 * NBD
ENTRIES = CELL + RCAP
LAG = 8
AHEAD = 4

VMEM = pl.BlockSpec(memory_space=pltpu.VMEM)
SMEM = pl.BlockSpec(memory_space=pltpu.SMEM)


def diagonal(rows):
    lane = lax.broadcasted_iota(jnp.int32, (8, B), 1)
    sub = lax.broadcasted_iota(jnp.int32, (8, B), 0)
    bit = 8
    while len(rows) > 1:
        high = (lane & bit) != 0
        rows = [jnp.where(high, b, a) for a, b in zip(rows[::2], rows[1::2])]
        bit *= 2
    return jnp.sum(jnp.where((lane & 7) == sub, rows[0], 0.0), axis=0, keepdims=True)


def lane_sums(acc):
    sums = jnp.sum(acc.reshape(B // 8, 8, B), axis=2, keepdims=True)
    return diagonal([jnp.broadcast_to(sums[k], (8, B)) for k in range(B // 8)])


def matrix_sums(acc):
    high = acc.astype(jnp.bfloat16)
    low = (acc - high.astype(F32)).astype(jnp.bfloat16)
    sums = jnp.dot(
        jnp.concatenate([high, low], axis=1),
        jnp.ones((2 * B, B), jnp.bfloat16),
        preferred_element_type=F32,
    )
    return diagonal([sums[8 * k : 8 * k + 8] for k in range(B // 8)])


def product(*pairs, sums=lane_sums):
    acc = None
    for mat, vec in pairs:
        term = mat * vec
        acc = term if acc is None else acc + term
    return sums(acc)


def row(ref, index):
    return ref[pl.ds(index, 1), :]


def at(ref, g):
    return ref[g : g + 1, :]


def send_rows(asked, values, send):
    for q in range(SLOTS):
        send[q : q + 1, :] = row(values, asked[q, 0])


def anchor_kernel(out):
    out[...] = jnp.zeros_like(out)


def list_kernel(own, margin, vert, cell, fetch, count, anchor, index, wish, live):
    def note(entry, value):
        index[entry : entry + 1, :] = jnp.full((1, B), value, jnp.int32)

    for g in range(NBD):
        note(OWN + g, own[0, g])
        note(OWN + NBD + g, own[1, g])
        note(MARGIN + g, margin[g])
        note(VERT + g, vert[g])
        peer = margin[g] // CAP
        note(WIDE + g, peer * PIECE + fetch[0, margin[g] % CAP, peer])
    for r in range(RCAP):
        note(CELL + r, cell[r])
    for q in range(SLOTS):
        wish[q : q + 1, :] = jnp.full((1, B), fetch[0, q % CAP, q // CAP], jnp.int32).astype(F32)
    slot = lax.broadcasted_iota(jnp.int32, (RCAP, B), 0)
    live[...] = (slot < count[0]).astype(F32)


def first_kernel(wish, pre, rhs, t_out, send):
    for g in range(NBD):
        t_out[g : g + 1, :] = product(
            (pre[g], at(rhs, g)), sums=matrix_sums if g % 2 else lane_sums
        )
    t = t_out[...]
    for p in range(TILES):
        send[PIECE * p : PIECE * p + NBD, :] = t
        send[PIECE * p + NBD : PIECE * (p + 1), :] = wish[CAP * p : CAP * (p + 1), :]


def staggered(fetch_row, first, second):
    held = {}
    for g in range(-AHEAD, NBD + LAG):
        if g + AHEAD < NBD:
            held[g + AHEAD] = fetch_row(g + AHEAD)
        if 0 <= g < NBD:
            first(g, held.pop(g))
        if g >= LAG:
            second(g - LAG)


def step_rows(index, near, near_at, diag, off, pre, t, res, w, finish):
    def rows_of(g):
        return index[OWN + g, 0], index[OWN + NBD + g, 0], index[near_at + g, 0]

    def extended(g, at_rows):
        w[g : g + 1, :] = at(res, g) - product(
            (diag[g], at(t, g)),
            (off[g, 0], row(t, at_rows[0])),
            (off[g, 1], row(t, at_rows[1])),
            (off[g, 2], row(near, at_rows[2])),
        )

    def turn(g):
        finish(
            g,
            at(t, g)
            + product((pre[g], at(w, g)), sums=matrix_sums if g % 4 == 1 else lane_sums),
        )

    staggered(rows_of, extended, turn)


def first_step_kernel(
    index, live, diag, off, pre, t, table, rhs, root_pre, root_rhs,
    s_out, send, asked, ur_out, w,
):
    for p in range(TILES):
        asked[CAP * p : CAP * (p + 1), :] = table[
            PIECE * p + NBD : PIECE * p + NBD + CAP, :
        ].astype(jnp.int32)

    def finish(g, z):
        s_out[g : g + 1, :] = z * (1.0 / THETA)

    step_rows(index, table, WIDE, diag, off, pre, t, rhs, w, finish)
    for r in range(RCAP):
        z = product((root_pre[r], at(root_rhs, r)), sums=matrix_sums)
        ur_out[r : r + 1, :] = jnp.where(at(live, r) > 0.0, z * (1.0 / THETA), 0.0)
    send_rows(asked, s_out, send)


def step_kernel(keep, gain, index, diag, off, pre, t, table, res, s_in, asked, s_out, send, w):
    def finish(g, z):
        s_out[g : g + 1, :] = keep * at(s_in, g) + gain * z

    step_rows(index, table, MARGIN, diag, off, pre, t, res, w, finish)
    send_rows(asked, s_out, send)


def residual_rows(index, diag, off, down, s, table, below, above, res, ur, r_out, after=None):
    r_out[...] = res[...]
    for r in range(RCAP):
        spot = pl.ds(index[CELL + r, 0], 1)
        r_out[spot, :] = r_out[spot, :] - product((down[r], at(ur, r)), sums=matrix_sums if after else lane_sums)

    def rows_of(g):
        return (
            index[OWN + g, 0], index[OWN + NBD + g, 0], index[MARGIN + g, 0], index[VERT + g, 0]
        )

    def applied(g, at_rows):
        vert = at_rows[3]
        over = jnp.where(vert < NBD, row(below, vert % NBD), row(above, vert % NBD))
        r_out[g : g + 1, :] = at(r_out, g) - product(
            (diag[g], at(s, g)),
            (off[g, 0], row(s, at_rows[0])),
            (off[g, 1], row(s, at_rows[1])),
            (off[g, 2], row(table, at_rows[2])),
            (off[g, 3], over),
        )

    staggered(rows_of, applied, after or (lambda g: None))


def residual_kernel(
    keep, gain, index, diag, off, pre, root_diag, root_pre, root_up, down,
    s, table, below, above, res, ur, rr, live, asked,
    t_out, r_out, ur_out, send, rr_out,
):
    def change_root(r):
        change = product(
            (root_diag[r], at(ur, r)), (root_up[r], row(s, index[CELL + r, 0])),
            sums=matrix_sums,
        )
        rr_out[r : r + 1, :] = at(rr, r) - change

    def turn_root(r):
        z = product((root_pre[r], at(rr_out, r)), sums=matrix_sums)
        ur_out[r : r + 1, :] = jnp.where(
            at(live, r) > 0.0, keep * at(ur, r) + gain * z, 0.0
        )

    def turn(g):
        t_out[g : g + 1, :] = product((pre[g], at(r_out, g)))
        if g % 2 == 0 and g < 2 * RCAP:
            change_root(g // 2)
        if g % 2 == 0 and g >= 2 * RCAP:
            turn_root(g // 2 - RCAP)

    residual_rows(index, diag, off, down, s, table, below, above, res, ur, r_out, turn)
    send_rows(asked, t_out, send)


def last_kernel(
    index, diag, off, down, s, table, below, above, res, ur, s_first, s_before, ur_first, ur_before,
    r_out, x_out, root_x,
):
    x_out[...] = s_first[...] + s_before[...] + s[...]
    root_x[...] = ur_first[...] + ur_before[...] + ur[...]
    residual_rows(index, diag, off, down, s, table, below, above, res, ur, r_out)


def call(kernel, name, scalars, arrays, outs, scratch=(), work=20_000_000_000):
    shapes = [s if isinstance(s, jax.ShapeDtypeStruct) else jax.ShapeDtypeStruct(s, F32) for s in outs]
    return pl.pallas_call(
        kernel,
        out_shape=tuple(shapes),
        in_specs=[SMEM] * len(scalars) + [VMEM] * len(arrays),
        out_specs=(VMEM,) * len(outs),
        scratch_shapes=[pltpu.VMEM(shape, F32) for shape in scratch],
        compiler_params=pltpu.CompilerParams(vmem_limit_bytes=4 * 2**20),
        cost_estimate=pl.CostEstimate(
            flops=work, transcendentals=0, bytes_accessed=work // 500
        ),
        name=name,
    )(*scalars, *arrays)


def body(
    soil_diag, soil_off, soil_pre, own_cols, margin_slot, vertical_col, fetch_rows, soil_rhs,
    root_diag, root_pre, root_up, root_down, root_cell, root_count, root_rhs,
):
    slabs = lax.axis_size("slab")
    own_cols, fetch_rows = own_cols.T, jnp.swapaxes(fetch_rows, 1, 2)
    soil, root, table = (NBD, B), (RCAP, B), (SLOTS, B)

    def exchange(rows):
        pieces = rows.reshape(TILES, -1, CAP, B)
        return lax.all_to_all(pieces, "tile", 0, 0).reshape(rows.shape)

    def vertical(s):
        up = [(i, (i + 1) % slabs) for i in range(slabs)]
        above = lax.ppermute(s, "slab", [(j, i) for i, j in up])
        return lax.ppermute(s, "slab", up), above

    (anchor,) = call(anchor_kernel, "anchor", (), (), (root,))
    entries = jax.ShapeDtypeStruct((ENTRIES, B), jnp.int32)
    index, wish, live = call(
        list_kernel, "lists",
        (own_cols, margin_slot, vertical_col, root_cell, fetch_rows, root_count),
        (anchor,), (entries, table, root), work=1000,
    )
    t, send = call(
        first_kernel, "first", (), (wish, soil_pre, soil_rhs), (soil, (TILES * PIECE, B))
    )
    got = exchange(send)
    s, send, asked, ur = call(
        first_step_kernel, "step0", (),
        (index, live, soil_diag, soil_off, soil_pre, t, got, soil_rhs, root_pre, root_rhs),
        (soil, table, jax.ShapeDtypeStruct(table, jnp.int32), root), (soil,),
    )
    r, rr, steps, urs = soil_rhs, root_rhs, [s], [ur]
    rho = 1.0 / SIGMA
    for sweep in range(SWEEPS):
        below, above = vertical(s)
        got = exchange(send)
        if sweep + 1 == SWEEPS:
            r, x, root_x = call(
                last_kernel, "last", (),
                (index, soil_diag, soil_off, root_down, s, got, below, above, r, ur, *steps[:2], *urs[:2]),
                (soil, soil, root),
            )
            break
        rho_new = 1.0 / (2.0 * SIGMA - rho)
        keep, gain = rho_new * rho, 2.0 * rho_new / DELTA
        rho = rho_new
        more = sweep + 2 < SWEEPS
        t, r, ur, send, *rest = call(
            functools.partial(residual_kernel, keep, gain), f"residual{sweep}", (),
            (index, soil_diag, soil_off, soil_pre, root_diag, root_pre, root_up, root_down,
             s, got, below, above, r, urs[-1], rr, live, asked),
            (soil, soil, root, table) + (root,) * more, (root,) * (not more),
        )
        rr = rest[0] if more else None
        urs.append(ur)
        got = exchange(send)
        s, send = call(
            functools.partial(step_kernel, keep, gain), f"step{sweep + 1}", (),
            (index, soil_diag, soil_off, soil_pre, t, got, r, s, asked),
            (soil, table), (soil,),
        )
        steps.append(s)
    return x, root_x, r


def solution(mesh):
    split = P(("slab", "tile"))
    return jax.shard_map(
        body, mesh=mesh, in_specs=(split,) * 15, out_specs=(split,) * 3, check_vma=False
    )
```
